512 devices in a mesh: row: 8 (over x, z_hi), col: 8 (over y, core), depth: 8 (over z_lo).
Axes of the slice: x: 4, y: 4, z: 16 (z_hi: 2, z_lo: 8; z = z_hi * 8 + z_lo), core: 2. Of those that a mesh axis runs over, the one named last changes fastest.
Arguments:
- inputs: bfloat16 [4096, 3072], P(('depth', 'row'), 'col'), may hold values from -6 to 6
- up_weight: bfloat16 [3072, 12288], P('col', 'row'), may hold values from -0.109375 to 0.109375
- down_weight: bfloat16 [12288, 3072], P('row', 'col'), may hold values from -0.0546875 to 0.0546875
- out_grad: bfloat16 [4096, 3072], P(('depth', 'row'), 'col'), may hold values from -6 to 6
Outputs:
- outputs: bfloat16 [4096, 3072], P(('depth', 'row'), 'col')
- in_grad: bfloat16 [4096, 3072], P(('depth', 'row'), 'col')
- up_grad: bfloat16 [3072, 12288], P('col', 'row')
- down_grad: bfloat16 [12288, 3072], P('row', 'col')
The draws below stay inside these ranges and needn't reach their ends.
All inputs are finite; a program needn't handle non-finite values.
Results may differ from the reference program's by a relative error of at most 0.028.
Values may be sent and summed in bfloat16 or wider, within the bound.
No kernel may reach another device: no remote copies, remote signals or barrier semaphores. Data moves between devices by JAX's collectives and lax.ppermute only.
A program may use at most 64 MiB of HBM per device.

```python
import jax
import jax.numpy as jnp
from jax import lax

D = 3072
FF = 12288
TOKENS = 4096
N_ROW = 8
N_COL = 8
N_DEPTH = 8


def levels(key, extent, split, smallest, high):
    loudness, own = 1.0, jax.random.fold_in(key, 6)
    for dim, blocks in split:
        steps = jnp.exp(jax.random.uniform(jax.random.fold_in(own, dim), (blocks,), jnp.float32, smallest / len(split), high / len(split)))
        loudness = loudness * jnp.repeat(steps, extent[dim] // blocks).reshape([-1 if axis == dim else 1 for axis in range(len(extent))])
    return loudness


def gaussian(rng, dims, spread, bound, shards=(), kind=jnp.bfloat16):
    loudness = levels(rng, dims, shards, -0.22, 0.18) if shards else 1.0
    values = jax.random.normal(rng, dims, jnp.float32) * spread * loudness
    return jnp.minimum(jnp.maximum(values, -bound), bound).astype(kind)


def setup_inputs(seed: int = 0) -> dict:
    splits = jax.random.split(jax.random.key(seed), 5)
    return {
        "inputs": gaussian(splits[0], (TOKENS, D), 1.0, 6.0, ((0, 64), (1, 8))),
        "up_weight": gaussian(splits[1], (D, FF), D ** -0.5, 0.109375, ((0, 8), (1, 8))),
        "down_weight": gaussian(splits[2], (FF, D), FF ** -0.5, 0.0546875, ((0, 8), (1, 8))),
        "out_grad": gaussian(splits[3], (TOKENS, D), 1.0, 6.0, ((0, 64), (1, 8))),
    }


def gelu_value(preact):
    wide = preact.astype(jnp.float32)
    return 0.5 * wide * (1.0 + jax.scipy.special.erf(wide * 0.7071067811865476))


def gelu_slope(preact):
    wide = preact.astype(jnp.float32)
    return 0.5 * (1.0 + jax.scipy.special.erf(wide * 0.7071067811865476)) + wide * jnp.exp(-0.5 * wide * wide) * 0.3989422804014327


def split_sum(left, right, pieces, factor):
    width = left.shape[1] // pieces

    def advance(total, index):
        start = (index * width).astype(jnp.int32)
        part_left = lax.dynamic_slice_in_dim(left, start, width, 1)
        part_right = lax.dynamic_slice_in_dim(right, start, width, 0)
        rounded = (jnp.dot(part_left, part_right, preferred_element_type=jnp.float32) * factor).astype(jnp.bfloat16)
        rounded = lax.optimization_barrier(rounded)
        return total + rounded.astype(jnp.float32), None

    initial = jnp.zeros((left.shape[0], right.shape[1]), jnp.float32)
    total, _ = lax.scan(advance, initial, jnp.arange(pieces, dtype=jnp.int32))
    return total


def reference(inputs, up_weight, down_weight, out_grad):
    loss_scale = float(TOKENS) ** -0.5
    preact = split_sum(inputs, up_weight, N_COL, 1.0).astype(jnp.bfloat16)
    act = gelu_value(preact).astype(jnp.bfloat16)
    outputs = split_sum(act, down_weight, N_ROW, 1.0).astype(jnp.bfloat16)
    act_grad = split_sum(out_grad, down_weight.T, N_COL, 1.0)
    hidden_grad = (act_grad * gelu_slope(preact)).astype(jnp.bfloat16)
    in_grad = split_sum(hidden_grad, up_weight.T, N_ROW, 1.0).astype(jnp.bfloat16)
    down_grad = split_sum(act.T, out_grad, N_DEPTH, loss_scale).astype(jnp.bfloat16)
    up_grad = split_sum(inputs.T, hidden_grad, N_DEPTH, loss_scale).astype(jnp.bfloat16)
    return outputs, in_grad, up_grad, down_grad
```

```python
import jax
import jax.numpy as jnp
from jax import lax
from jax.sharding import Mesh
from jax.sharding import PartitionSpec as P

F32 = jnp.float32
BF16 = jnp.bfloat16


def gelu_value(wide):
    return 0.5 * wide * (1.0 + jax.scipy.special.erf(wide * 0.7071067811865476))


def gelu_slope(wide):
    return (
        0.5 * (1.0 + jax.scipy.special.erf(wide * 0.7071067811865476))
        + wide * jnp.exp(-0.5 * wide * wide) * 0.3989422804014327
    )


def contract(left, right, dims):
    return lax.dot_general(left, right, (dims, ((), ())), preferred_element_type=F32)


def scatter_sum(values, axis):
    count = lax.axis_size(axis)
    parts = lax.all_to_all(values, axis, 0, 0, tiled=True)
    parts = parts.reshape((count, parts.shape[0] // count) + parts.shape[1:])
    return jnp.sum(parts.astype(F32), axis=0)


def spread(values, axis):
    count = lax.axis_size(axis)
    copies = jnp.broadcast_to(values[None], (count,) + values.shape)
    return lax.all_to_all(copies.reshape((-1,) + values.shape[1:]), axis, 0, 0, tiled=True)


def other_half(values):
    depth = lax.axis_size("d")
    pairs = [
        (h * depth + d, (1 - h) * depth + (d + depth // 2) % depth)
        for h in range(2)
        for d in range(depth)
    ]
    return lax.ppermute(values, ("h", "d"), pairs)


def on_device(inputs, up_weight, down_weight, out_grad):
    hidden = up_weight.shape[1]
    features = inputs.shape[1]
    own = inputs.shape[0]
    tokens = own * 64
    loss_scale = float(tokens) ** (-0.5)

    rows = jnp.concatenate([inputs, out_grad], axis=1)
    rows = jnp.concatenate([rows, other_half(rows)], axis=0)
    rows = lax.all_gather(rows, "x", axis=0, tiled=True)
    every_input, every_grad = rows[:, :features], rows[:, features:]

    partial = jnp.concatenate(
        [
            contract(every_input, up_weight, ((1,), (0,))).astype(BF16),
            contract(every_grad, down_weight, ((1,), (1,))).astype(BF16),
        ],
        axis=1,
    )
    partial = scatter_sum(partial, "k").astype(BF16)
    sums = scatter_sum(partial, "y")
    preact = sums[:, :hidden].astype(BF16).astype(F32)
    act = gelu_value(preact).astype(BF16)
    hidden_grad = (sums[:, hidden:] * gelu_slope(preact)).astype(BF16)
    both = jnp.concatenate([act, hidden_grad], axis=1)
    both = spread(spread(both, "y"), "k")
    every_act, every_hidden = both[:, :hidden], both[:, hidden:]

    down_term = (loss_scale * contract(every_act, every_grad, ((0,), (0,)))).astype(BF16)
    up_term = (loss_scale * contract(every_input, every_hidden, ((0,), (0,)))).astype(BF16)
    up_grad, down_grad = lax.psum((up_term, down_term), "d")

    features_part = jnp.concatenate(
        [
            contract(every_act, down_weight, ((1,), (0,))).astype(BF16),
            contract(every_hidden, up_weight, ((1,), (1,))).astype(BF16),
        ],
        axis=1,
    )
    mine = scatter_sum(features_part, "x")
    total = mine[:own] + other_half(mine[own:].astype(BF16)).astype(F32)
    total = total.astype(BF16)
    return total[:, :features], total[:, features:], up_grad, down_grad


def solution(mesh):
    split = Mesh(mesh.devices.reshape(4, 2, 4, 2, 8), ("x", "h", "y", "k", "d"))
    rows = P(("d", "x", "h"), ("y", "k"))
    up = P(("y", "k"), ("x", "h"))
    down = P(("x", "h"), ("y", "k"))
    return jax.shard_map(
        on_device,
        mesh=split,
        in_specs=(rows, up, down, rows),
        out_specs=(rows, rows, up, down),
        check_vma=False,
    )
```

```python
import jax
import jax.numpy as jnp
from jax import lax
from jax.sharding import Mesh
from jax.sharding import PartitionSpec as P

F32 = jnp.float32
BF16 = jnp.bfloat16


def gelu_value(wide):
    return 0.5 * wide * (1.0 + jax.scipy.special.erf(wide * 0.7071067811865476))


def gelu_slope(wide):
    return (
        0.5 * (1.0 + jax.scipy.special.erf(wide * 0.7071067811865476))
        + wide * jnp.exp(-0.5 * wide * wide) * 0.3989422804014327
    )


def contract(left, right, dims):
    return lax.dot_general(left, right, (dims, ((), ())), preferred_element_type=F32)


def scatter_sum(values, axis):
    count = lax.axis_size(axis)
    parts = lax.all_to_all(values, axis, 0, 0, tiled=True)
    parts = parts.reshape((count, parts.shape[0] // count) + parts.shape[1:])
    return jnp.sum(parts.astype(F32), axis=0)


def spread(values, axis):
    count = lax.axis_size(axis)
    copies = jnp.broadcast_to(values[None], (count,) + values.shape)
    return lax.all_to_all(copies.reshape((-1,) + values.shape[1:]), axis, 0, 0, tiled=True)


def on_device(inputs, up_weight, down_weight, out_grad):
    own, features = inputs.shape
    half = up_weight.shape[1] // 2
    start = lax.axis_index("e") * half
    up_half = lax.dynamic_slice_in_dim(up_weight, start, half, 1)
    down_half = lax.dynamic_slice_in_dim(down_weight, start, half, 0)
    loss_scale = float(own * 64) ** (-0.5)

    rows = jnp.concatenate([inputs, out_grad], axis=1)
    rows = lax.all_gather(rows, ("h", "e"), axis=0, tiled=True)
    rows = spread(rows, "x")
    every_input, every_grad = rows[:, :features], rows[:, features:]

    partial = jnp.concatenate(
        [
            contract(every_input, up_half, ((1,), (0,))).astype(BF16),
            contract(every_grad, down_half, ((1,), (1,))).astype(BF16),
        ],
        axis=1,
    )
    partial = scatter_sum(partial, "k").astype(BF16)
    sums = scatter_sum(partial, "y")
    preact = sums[:, :half].astype(BF16).astype(F32)
    act = gelu_value(preact).astype(BF16)
    hidden_grad = (sums[:, half:] * gelu_slope(preact)).astype(BF16)
    both = jnp.concatenate([act, hidden_grad], axis=1)
    both = spread(spread(both, "y"), "k")
    every_act, every_hidden = both[:, :half], both[:, half:]

    down_term = (loss_scale * contract(every_act, every_grad, ((0,), (0,)))).astype(BF16)
    up_term = (loss_scale * contract(every_input, every_hidden, ((0,), (0,)))).astype(BF16)
    up_piece = scatter_sum(up_term, "l").astype(BF16)
    down_piece = scatter_sum(down_term, "l").astype(BF16)
    piece = jnp.concatenate([up_piece[:, :features], up_piece[:, features:], down_piece], axis=0)
    pieces = lax.all_gather(piece, ("e", "l"), axis=0, tiled=False)
    quarter = features // 4
    pieces = pieces.reshape(2, 4, 4 * quarter, features)
    up_grad = pieces[:, :, : 2 * quarter].reshape(2, 4, 2, quarter, features)
    up_grad = up_grad.transpose(1, 3, 0, 2, 4).reshape(features, 2 * half)
    down_grad = pieces[:, :, 2 * quarter :].reshape(2 * half, features)

    features_part = jnp.concatenate(
        [
            contract(every_act, down_half, ((1,), (0,))).astype(BF16),
            contract(every_hidden, up_half, ((1,), (1,))).astype(BF16),
        ],
        axis=1,
    )
    total = scatter_sum(features_part, "x").astype(BF16)
    total = scatter_sum(total, ("h", "e")).astype(BF16)
    return total[:, :features], total[:, features:], up_grad, down_grad


def solution(mesh):
    split = Mesh(mesh.devices.reshape(4, 2, 4, 2, 2, 4), ("x", "h", "y", "k", "e", "l"))
    rows = P(("e", "l", "x", "h"), ("y", "k"))
    up = P(("y", "k"), ("x", "h"))
    down = P(("x", "h"), ("y", "k"))
    return jax.shard_map(
        on_device,
        mesh=split,
        in_specs=(rows, up, down, rows),
        out_specs=(rows, rows, up, down),
        check_vma=False,
    )
```

```python
import jax
import jax.numpy as jnp
from jax import lax
from jax.experimental import pallas as pl
from jax.experimental.pallas import tpu as pltpu
from jax.sharding import Mesh
from jax.sharding import PartitionSpec as P

F32 = jnp.float32
BF16 = jnp.bfloat16

FOLDED = [0, 2, 4, 6, 7, 5, 3, 1]


def gelu_value(wide):
    return 0.5 * wide * (1.0 + jax.scipy.special.erf(wide * 0.7071067811865476))


def gelu_slope(wide):
    return (
        0.5 * (1.0 + jax.scipy.special.erf(wide * 0.7071067811865476))
        + wide * jnp.exp(-0.5 * wide * wide) * 0.3989422804014327
    )


def contract(left, right, dims):
    return lax.dot_general(left, right, (dims, ((), ())), preferred_element_type=F32)


def scatter_sum(values, axis):
    count = lax.axis_size(axis)
    parts = lax.all_to_all(values, axis, 0, 0, tiled=True)
    parts = parts.reshape((count, parts.shape[0] // count) + parts.shape[1:])
    return jnp.sum(parts.astype(F32), axis=0)


def gather(values, axis):
    return lax.all_gather(values, axis, axis=0, tiled=True)


def other_core(values):
    return lax.ppermute(values, "k", [(0, 1), (1, 0)])


def after(values, earlier):
    return lax.optimization_barrier((values, earlier))[0]


def place_kernel(pieces, up, down, sems):
    copies = []
    features = down.shape[1]
    quarter = features // 4
    for slot, source in enumerate(FOLDED):
        e, l = source // 4, source % 4
        for side in range(2):
            rows, cols = l * quarter, (2 * e + side) * features
            copies.append(
                (
                    pieces.at[slot, pl.ds(side * quarter, quarter)],
                    up.at[pl.ds(rows, quarter), pl.ds(cols, features)],
                )
            )
        copies.append(
            (
                pieces.at[slot, pl.ds(2 * quarter, 2 * quarter)],
                down.at[pl.ds(source * 2 * quarter, 2 * quarter)],
            )
        )
    copies = [pltpu.make_async_copy(*pair, sems.at[i]) for i, pair in enumerate(copies)]
    for copy in copies:
        copy.start()
    for copy in copies:
        copy.wait()


def place(pieces):
    features = pieces.shape[2]
    vmem = pl.BlockSpec(memory_space=pltpu.VMEM)
    return pl.pallas_call(
        place_kernel,
        out_shape=(
            jax.ShapeDtypeStruct((features, 4 * features), BF16),
            jax.ShapeDtypeStruct((4 * features, features), BF16),
        ),
        in_specs=[pl.BlockSpec(memory_space=pl.ANY)],
        out_specs=(vmem, vmem),
        scratch_shapes=[pltpu.SemaphoreType.DMA((3 * len(FOLDED),))],
    )(pieces)


def on_device(inputs, up_weight, down_weight, out_grad):
    own, features = inputs.shape
    core = lax.axis_index("k")
    half = up_weight.shape[1] // 2
    start = lax.axis_index("e") * half
    up_half = lax.dynamic_slice_in_dim(up_weight, start, half, 1)
    down_half = lax.dynamic_slice_in_dim(down_weight, start, half, 0)
    loss_scale = float(own * 64) ** (-0.5)

    rows = jnp.concatenate([inputs, out_grad], axis=1)
    swapped = jnp.concatenate([rows[own // 2 :], rows[: own // 2]], axis=0)
    rows = gather(jnp.where(core == 0, rows, swapped), ("h", "e"))

    def split(gathered):
        blocks = gathered.reshape(-1, 2, own // 2, features)
        return [blocks[:, side].reshape(-1, features) for side in range(2)]

    my_input, far_input = split(gather(rows[:, :features], "x"))

    far = contract(far_input, up_half, ((1,), (0,))).astype(BF16)
    part = contract(my_input, up_half, ((1,), (0,))) + other_core(far).astype(F32)
    part = part.astype(BF16)
    preact_sum = scatter_sum(part, "y")

    grad_rows = after(rows[:, features:], part)
    my_grad, far_grad = split(after(gather(grad_rows, "x"), preact_sum))
    far = contract(far_grad, down_half, ((1,), (1,))).astype(BF16)
    part = contract(my_grad, down_half, ((1,), (1,))) + other_core(far).astype(F32)
    part = part.astype(BF16)
    act_grad = scatter_sum(part, "y")

    preact = preact_sum.astype(BF16).astype(F32)
    my_act, act_grad, preact = lax.optimization_barrier(
        (gather(gelu_value(preact).astype(BF16), "y"), act_grad, preact)
    )
    far_act = other_core(my_act)
    down_term = loss_scale * (
        contract(my_act, my_grad, ((0,), (0,))) + contract(far_act, far_grad, ((0,), (0,)))
    )
    down_term = down_term.astype(BF16)
    down_piece = scatter_sum(down_term, "l").astype(BF16)

    hidden_grad = (act_grad * gelu_slope(preact)).astype(BF16)
    my_hidden = gather(after(hidden_grad, down_term), "y")
    far_hidden = other_core(my_hidden)
    up_term = loss_scale * (
        contract(my_input, my_hidden, ((0,), (0,))) + contract(far_input, far_hidden, ((0,), (0,)))
    )
    up_piece = scatter_sum(up_term.astype(BF16), "l").astype(BF16)

    piece = jnp.concatenate([up_piece[:, :features], up_piece[:, features:], down_piece], axis=0)
    pieces = lax.all_gather(piece, ("e", "l"), axis_index_groups=[FOLDED])
    up_grad, down_grad = place(pieces)
    my_act, my_hidden, far_act, far_hidden, _ = lax.optimization_barrier(
        (my_act, my_hidden, far_act, far_hidden, piece)
    )

    blocks = 16
    sides = []
    for act, hidden in ((my_act, my_hidden), (far_act, far_hidden)):
        side = jnp.concatenate(
            [
                contract(act, down_half, ((1,), (0,))).astype(BF16),
                contract(hidden, up_half, ((1,), (1,))).astype(BF16),
            ],
            axis=1,
        )
        sides.append(side.reshape(blocks, own // 2, 2 * features))
    total = jnp.stack(sides, axis=1).reshape(blocks * own, 2 * features)
    total = scatter_sum(total, "x").astype(BF16)
    total = scatter_sum(total, ("h", "e")).astype(BF16)
    swapped = jnp.concatenate([total[own // 2 :], total[: own // 2]], axis=0)
    total = jnp.where(core == 0, total, swapped)
    return total[:, :features], total[:, features:], up_grad, down_grad


def solution(mesh):
    split = Mesh(mesh.devices.reshape(4, 2, 4, 2, 2, 4), ("x", "h", "y", "k", "e", "l"))
    rows = P(("e", "l", "x", "h"), ("y", "k"))
    up = P(("y", "k"), ("x", "h"))
    down = P(("x", "h"), ("y", "k"))
    return jax.shard_map(
        on_device,
        mesh=split,
        in_specs=(rows, up, down, rows),
        out_specs=(rows, rows, up, down),
        check_vma=False,
    )
```

```python
import jax
import jax.numpy as jnp
from jax import lax
from jax.experimental import pallas as pl
from jax.experimental.pallas import tpu as pltpu
from jax.sharding import Mesh
from jax.sharding import PartitionSpec as P

F32 = jnp.float32
BF16 = jnp.bfloat16

FOLDED = [0, 2, 4, 6, 7, 5, 3, 1]


def gelu_value(wide):
    return 0.5 * wide * (1.0 + jax.scipy.special.erf(wide * 0.7071067811865476))


def gelu_slope(wide):
    return (
        0.5 * (1.0 + jax.scipy.special.erf(wide * 0.7071067811865476))
        + wide * jnp.exp(-0.5 * wide * wide) * 0.3989422804014327
    )


def contract(left, right, dims):
    return lax.dot_general(left, right, (dims, ((), ())), preferred_element_type=F32)


def scatter_sum(values, axis):
    count = lax.axis_size(axis)
    parts = lax.all_to_all(values, axis, 0, 0, tiled=True)
    parts = parts.reshape((count, parts.shape[0] // count) + parts.shape[1:])
    return jnp.sum(parts.astype(F32), axis=0)


def gather(values, axis):
    return lax.all_gather(values, axis, axis=0, tiled=True)


def other_core(values):
    return lax.ppermute(values, "k", [(0, 1), (1, 0)])


def after(values, earlier):
    return lax.optimization_barrier((values, earlier))[0]


def place_kernel(pieces, up, down, sems):
    copies = []
    features = down.shape[1]
    quarter = features // 4
    for slot, source in enumerate(FOLDED):
        e, l = source // 4, source % 4
        for side in range(2):
            rows, cols = l * quarter, (2 * e + side) * features
            copies.append(
                (
                    pieces.at[slot, pl.ds(side * quarter, quarter)],
                    up.at[pl.ds(rows, quarter), pl.ds(cols, features)],
                )
            )
        copies.append(
            (
                pieces.at[slot, pl.ds(2 * quarter, 2 * quarter)],
                down.at[pl.ds(source * 2 * quarter, 2 * quarter)],
            )
        )
    copies = [pltpu.make_async_copy(*pair, sems.at[i]) for i, pair in enumerate(copies)]
    for copy in copies:
        copy.start()
    for copy in copies:
        copy.wait()


def place(pieces):
    features = pieces.shape[2]
    vmem = pl.BlockSpec(memory_space=pltpu.VMEM)
    return pl.pallas_call(
        place_kernel,
        out_shape=(
            jax.ShapeDtypeStruct((features, 4 * features), BF16),
            jax.ShapeDtypeStruct((4 * features, features), BF16),
        ),
        in_specs=[pl.BlockSpec(memory_space=pl.ANY)],
        out_specs=(vmem, vmem),
        scratch_shapes=[pltpu.SemaphoreType.DMA((3 * len(FOLDED),))],
    )(pieces)


def on_device(inputs, up_weight, down_weight, out_grad):
    own, features = inputs.shape
    side = lax.axis_index("k")
    half = up_weight.shape[1] // 2
    start = lax.axis_index("e") * half
    up_half = lax.dynamic_slice_in_dim(up_weight, start, half, 1)
    down_half = lax.dynamic_slice_in_dim(down_weight, start, half, 0)
    loss_scale = float(own * 64) ** (-0.5)

    def half_rows(which):
        return jnp.concatenate(
            [
                lax.dynamic_slice_in_dim(values, which * (own // 2), own // 2, 0)
                for values in (inputs, out_grad)
            ],
            axis=1,
        )

    kept, received = half_rows(side), other_core(half_rows(1 - side))
    up_half, down_half = after((up_half, down_half), received)
    up_both = jnp.concatenate([up_half, other_core(up_half)], axis=0)
    down_far = other_core(down_half)
    rows = jnp.concatenate(
        [
            kept[:, :features],
            received[:, :features],
            kept[:, features:],
            received[:, features:],
        ],
        axis=1,
    )
    rows = gather(after(rows, (up_half, down_half)), ("h", "e"))

    every_input = gather(rows[:, : 2 * features], "x")
    part = contract(every_input, up_both, ((1,), (0,))).astype(BF16)
    preact_sum = scatter_sum(part, "y")

    every_grad = after(gather(after(rows[:, 2 * features :], part), "x"), preact_sum)
    my_grad, far_grad = every_grad[:, :features], every_grad[:, features:]
    part = contract(my_grad, down_half, ((1,), (1,))) + contract(far_grad, down_far, ((1,), (1,)))
    part = part.astype(BF16)
    act_grad = scatter_sum(part, "y")

    preact = preact_sum.astype(BF16).astype(F32)
    act, act_grad, preact = lax.optimization_barrier(
        (gather(gelu_value(preact).astype(BF16), "y"), act_grad, preact)
    )
    far = contract(act, far_grad, ((0,), (0,))).astype(BF16)
    down_term = contract(act, my_grad, ((0,), (0,))) + other_core(far).astype(F32)
    down_term = (loss_scale * down_term).astype(BF16)
    down_piece = scatter_sum(down_term, "l").astype(BF16)

    hidden_grad = (act_grad * gelu_slope(preact)).astype(BF16)
    hidden = gather(after(hidden_grad, down_term), "y")
    far = contract(every_input[:, features:], hidden, ((0,), (0,))).astype(BF16)
    up_term = contract(every_input[:, :features], hidden, ((0,), (0,))) + other_core(far).astype(F32)
    up_term = (loss_scale * up_term).astype(BF16)
    up_piece = scatter_sum(up_term, "l").astype(BF16)

    piece = jnp.concatenate([up_piece[:, :features], up_piece[:, features:], down_piece], axis=0)
    pieces = lax.all_gather(piece, ("e", "l"), axis_index_groups=[FOLDED])
    up_grad, down_grad = place(pieces)

    act, hidden, _ = lax.optimization_barrier((act, hidden, up_term))
    total = jnp.concatenate(
        [
            contract(act, down_half, ((1,), (0,))).astype(BF16),
            contract(act, down_far, ((1,), (0,))).astype(BF16),
            contract(hidden, up_both, ((1,), (1,))).astype(BF16),
        ],
        axis=1,
    )
    total = scatter_sum(after(total, piece), "x").astype(BF16)
    total = scatter_sum(total, ("h", "e")).astype(BF16)
    kept = jnp.concatenate([total[:, :features], total[:, 2 * features : 3 * features]], axis=1)
    received = other_core(
        jnp.concatenate([total[:, features : 2 * features], total[:, 3 * features :]], axis=1)
    )
    total = jnp.where(
        side == 0,
        jnp.concatenate([kept, received], axis=0),
        jnp.concatenate([received, kept], axis=0),
    )
    return total[:, :features], total[:, features:], up_grad, down_grad


def solution(mesh):
    split = Mesh(mesh.devices.reshape(4, 2, 4, 2, 2, 4), ("x", "h", "y", "k", "e", "l"))
    rows = P(("e", "l", "x", "h"), ("y", "k"))
    up = P(("y", "k"), ("x", "h"))
    down = P(("x", "h"), ("y", "k"))
    return jax.shard_map(
        on_device,
        mesh=split,
        in_specs=(rows, up, down, rows),
        out_specs=(rows, rows, up, down),
        check_vma=False,
    )
```

```python
import jax
import jax.numpy as jnp
from jax import lax
from jax.experimental import pallas as pl
from jax.experimental.pallas import tpu as pltpu
from jax.sharding import Mesh
from jax.sharding import PartitionSpec as P

F32 = jnp.float32
BF16 = jnp.bfloat16
F16 = jnp.float16

FOLDED = [0, 2, 4, 6, 7, 5, 3, 1]


def gelu_value(wide):
    return 0.5 * wide * (1.0 + jax.scipy.special.erf(wide * 0.7071067811865476))


def gelu_slope(wide):
    return (
        0.5 * (1.0 + jax.scipy.special.erf(wide * 0.7071067811865476))
        + wide * jnp.exp(-0.5 * wide * wide) * 0.3989422804014327
    )


def contract(left, right, dims):
    return lax.dot_general(left, right, (dims, ((), ())), preferred_element_type=F32)


def scatter_sum(values, axis):
    count = lax.axis_size(axis)
    parts = lax.all_to_all(values, axis, 0, 0, tiled=True)
    parts = parts.reshape((count, parts.shape[0] // count) + parts.shape[1:])
    return jnp.sum(parts.astype(F32), axis=0)


def gather(values, axis):
    return lax.all_gather(values, axis, axis=0, tiled=True)


def other_core(values):
    return lax.ppermute(values, "k", [(0, 1), (1, 0)])


def after(values, earlier):
    return lax.optimization_barrier((values, earlier))[0]


def feature_kernel(act, hidden, down, up, *rest):
    out = rest[-1]
    features = down.shape[1]
    rows = act.shape[0] // 4
    for block in range(4):
        here = pl.ds(block * rows, rows)
        values = (
            contract(act[here], down[...], ((1,), (0,))).astype(BF16),
            contract(hidden[here], up[...], ((1,), (1,))).astype(BF16),
        )
        for side, value in enumerate(values):
            columns = pl.ds(side * features, features)
            if len(rest) == 1:
                out[here, columns] = value
            else:
                out[block, pl.ds(0, rows), columns] = value
        if len(rest) == 2:
            out[block, pl.ds(rows, rows)] = rest[0][here]


def feature_values(act, hidden, down, up, *more):
    rows, depth = act.shape
    features = down.shape[1]
    shape = (4, rows // 2, 2 * features) if more else (rows, 2 * features)
    return pl.pallas_call(
        feature_kernel,
        out_shape=jax.ShapeDtypeStruct(shape, BF16),
        cost_estimate=pl.CostEstimate(
            flops=4 * rows * depth * features,
            bytes_accessed=4 * rows * depth + 8 * depth * features,
            transcendentals=0,
        ),
    )(act, hidden, down, up, *more)


def pack(piece):
    wide = piece.astype(F32)
    top = jnp.maximum(jnp.max(jnp.abs(wide)), 1e-37)
    power = jnp.clip(14.0 - jnp.ceil(jnp.log2(top)), -20.0, 120.0)
    scaled = (wide * jnp.exp2(power)).astype(F16)
    return jnp.concatenate([scaled, jnp.full((16, piece.shape[1]), power).astype(F16)], axis=0)


def unpack(packed):
    rows = packed.shape[1] - 16
    power = packed[:, rows:, :1].astype(F32)[:, :1]
    return (packed[:, :rows].astype(F32) * jnp.exp2(-power)).astype(BF16)


def place_kernel(pieces, up, down, sems):
    copies = []
    features = down.shape[1]
    quarter = features // 4
    for slot, source in enumerate(FOLDED):
        e, l = source // 4, source % 4
        for side in range(2):
            rows, cols = l * quarter, (2 * e + side) * features
            copies.append(
                (
                    pieces.at[slot, pl.ds(side * quarter, quarter)],
                    up.at[pl.ds(rows, quarter), pl.ds(cols, features)],
                )
            )
        copies.append(
            (
                pieces.at[slot, pl.ds(2 * quarter, 2 * quarter)],
                down.at[pl.ds(source * 2 * quarter, 2 * quarter)],
            )
        )
    copies = [pltpu.make_async_copy(*pair, sems.at[i]) for i, pair in enumerate(copies)]
    for copy in copies:
        copy.start()
    for copy in copies:
        copy.wait()


def place(pieces):
    features = pieces.shape[2]
    vmem = pl.BlockSpec(memory_space=pltpu.VMEM)
    return pl.pallas_call(
        place_kernel,
        out_shape=(
            jax.ShapeDtypeStruct((features, 4 * features), BF16),
            jax.ShapeDtypeStruct((4 * features, features), BF16),
        ),
        in_specs=[pl.BlockSpec(memory_space=pl.ANY)],
        out_specs=(vmem, vmem),
        scratch_shapes=[pltpu.SemaphoreType.DMA((3 * len(FOLDED),))],
    )(pieces)


def on_device(inputs, up_weight, down_weight, out_grad):
    own, features = inputs.shape
    side = lax.axis_index("k")
    half = up_weight.shape[1] // 2
    start = lax.axis_index("e") * half
    up_half = lax.dynamic_slice_in_dim(up_weight, start, half, 1)
    down_half = lax.dynamic_slice_in_dim(down_weight, start, half, 0)
    loss_scale = float(own * 64) ** (-0.5)

    def half_rows(which):
        return jnp.concatenate(
            [
                lax.dynamic_slice_in_dim(values, which * (own // 2), own // 2, 0)
                for values in (inputs, out_grad)
            ],
            axis=1,
        )

    kept, received = half_rows(side), other_core(half_rows(1 - side))
    up_half, down_half = after((up_half, down_half), received)
    up_far = other_core(up_half)
    up_both = jnp.concatenate([up_half, up_far], axis=0)
    down_far = other_core(down_half)
    rows = jnp.concatenate(
        [
            kept[:, :features],
            received[:, :features],
            kept[:, features:],
            received[:, features:],
        ],
        axis=1,
    )
    rows = gather(after(rows, (up_half, down_half)), ("h", "e"))

    every_input = gather(rows[:, : 2 * features], "x")
    part = contract(every_input, up_both, ((1,), (0,))).astype(BF16)
    preact_sum = scatter_sum(part, "y")

    every_grad = after(gather(after(rows[:, 2 * features :], part), "x"), preact_sum)
    my_grad, far_grad = every_grad[:, :features], every_grad[:, features:]
    part = contract(my_grad, down_half, ((1,), (1,))) + contract(far_grad, down_far, ((1,), (1,)))
    part = part.astype(BF16)
    act_grad = scatter_sum(part, "y")

    preact = preact_sum.astype(BF16).astype(F32)
    act, act_grad, preact = lax.optimization_barrier(
        (gather(gelu_value(preact).astype(BF16), "y"), act_grad, preact)
    )
    far = contract(act, far_grad, ((0,), (0,))).astype(BF16)
    down_term = contract(act, my_grad, ((0,), (0,))) + other_core(far).astype(F32)
    down_term = (loss_scale * down_term).astype(BF16)
    down_piece = scatter_sum(down_term, "l").astype(BF16)

    hidden_grad = (act_grad * gelu_slope(preact)).astype(BF16)
    hidden = gather(after(hidden_grad, down_term), "y")
    far = contract(every_input[:, features:], hidden, ((0,), (0,))).astype(BF16)
    up_term = contract(every_input[:, :features], hidden, ((0,), (0,))) + other_core(far).astype(F32)
    up_term = (loss_scale * up_term).astype(BF16)

    act, hidden = after((act, hidden), up_term)
    far = other_core(feature_values(act, hidden, down_far, up_far))
    total = feature_values(act, hidden, down_half, up_half, far)
    total = total.reshape(16 * own, 2 * features)
    up_parts = after(lax.all_to_all(up_term, "l", 0, 0, tiled=True), total)
    up_piece = jnp.sum(up_parts.reshape(4, -1, half).astype(F32), axis=0).astype(BF16)
    piece = jnp.concatenate([up_piece[:, :features], up_piece[:, features:], down_piece], axis=0)
    packed = pack(piece)
    pieces = lax.all_gather(packed, ("e", "l"), axis_index_groups=[FOLDED])
    total, pieces = lax.optimization_barrier(
        (scatter_sum(after(total, packed), "x").astype(BF16), pieces)
    )
    up_grad, down_grad = place(unpack(pieces))
    total = total.reshape(2, 4, own // 2, 2 * features).transpose(1, 0, 2, 3)
    total = scatter_sum(total.reshape(4 * own, 2 * features), ("h", "e")).astype(BF16)
    total = after(total, (up_grad, down_grad))
    swapped = jnp.concatenate([total[own // 2 :], total[: own // 2]], axis=0)
    total = jnp.where(side == 0, total, swapped)
    return total[:, :features], total[:, features:], up_grad, down_grad


def solution(mesh):
    split = Mesh(mesh.devices.reshape(4, 2, 4, 2, 2, 4), ("x", "h", "y", "k", "e", "l"))
    rows = P(("e", "l", "x", "h"), ("y", "k"))
    up = P(("y", "k"), ("x", "h"))
    down = P(("x", "h"), ("y", "k"))
    return jax.shard_map(
        on_device,
        mesh=split,
        in_specs=(rows, up, down, rows),
        out_specs=(rows, rows, up, down),
        check_vma=False,
    )
```

```python
import jax
import jax.numpy as jnp
from jax import lax
from jax.experimental import pallas as pl
from jax.experimental.pallas import tpu as pltpu
from jax.sharding import Mesh
from jax.sharding import PartitionSpec as P

F32 = jnp.float32
BF16 = jnp.bfloat16
F16 = jnp.float16

FOLDED = [0, 2, 4, 6, 7, 5, 3, 1]


def gelu_value(wide):
    return 0.5 * wide * (1.0 + jax.scipy.special.erf(wide * 0.7071067811865476))


def gelu_slope(wide):
    return (
        0.5 * (1.0 + jax.scipy.special.erf(wide * 0.7071067811865476))
        + wide * jnp.exp(-0.5 * wide * wide) * 0.3989422804014327
    )


def contract(left, right, dims):
    return lax.dot_general(left, right, (dims, ((), ())), preferred_element_type=F32)


def scatter_sum(values, axis):
    count = lax.axis_size(axis)
    parts = lax.all_to_all(values, axis, 0, 0, tiled=True)
    parts = parts.reshape((count, parts.shape[0] // count) + parts.shape[1:])
    return jnp.sum(parts.astype(F32), axis=0)


def gather(values, axis):
    return lax.all_gather(values, axis, axis=0, tiled=True)


def other_core(values):
    return lax.ppermute(values, "k", [(0, 1), (1, 0)])


def after(values, earlier):
    return lax.optimization_barrier((values, earlier))[0]


def feature_kernel(act, hidden, weights, *rest):
    out = rest[-1]
    features = weights.shape[1] // 2
    rows = act.shape[0] // 4
    low, high = pl.ds(0, features), pl.ds(features, features)
    for columns in (low, high):
        if columns is low:
            values = contract(act[...], weights[:, low], ((1,), (0,)))
        else:
            values = contract(hidden[:, low], weights[low, high], ((1,), (1,)))
            values += contract(hidden[:, high], weights[high, high], ((1,), (1,)))
        values = values.astype(BF16)
        if len(rest) == 1:
            out[:, columns] = values
        else:
            for block in range(4):
                out[block, pl.ds(0, rows), columns] = values[block * rows : (block + 1) * rows]
    if len(rest) == 2:
        for block in range(4):
            out[block, pl.ds(rows, rows)] = rest[0][pl.ds(block * rows, rows)]


def feature_values(act, hidden, weights, *more):
    rows, depth = act.shape
    shape = (4, rows // 2, depth) if more else (rows, depth)
    return pl.pallas_call(
        feature_kernel,
        out_shape=jax.ShapeDtypeStruct(shape, BF16),
        cost_estimate=pl.CostEstimate(
            flops=2 * rows * depth * depth,
            bytes_accessed=6 * rows * depth + 2 * depth * depth,
            transcendentals=0,
        ),
    )(act, hidden, weights, *more)


def pack(piece):
    wide = piece.astype(F32)
    top = jnp.maximum(jnp.max(jnp.abs(wide)), 1e-37)
    power = jnp.clip(14.0 - jnp.ceil(jnp.log2(top)), -20.0, 120.0)
    scaled = (wide * jnp.exp2(power)).astype(F16)
    return jnp.concatenate([scaled, jnp.full((16, piece.shape[1]), power).astype(F16)], axis=0)


def unpack(packed):
    rows = packed.shape[1] - 16
    power = packed[:, rows:, :1].astype(F32)[:, :1]
    return (packed[:, :rows].astype(F32) * jnp.exp2(-power)).astype(BF16)


def place_kernel(pieces, up, down, sems):
    copies = []
    features = down.shape[1]
    quarter = features // 4
    for slot, source in enumerate(FOLDED):
        e, l = source // 4, source % 4
        for side in range(2):
            rows, cols = l * quarter, (2 * e + side) * features
            copies.append(
                (
                    pieces.at[slot, pl.ds(side * quarter, quarter)],
                    up.at[pl.ds(rows, quarter), pl.ds(cols, features)],
                )
            )
        copies.append(
            (
                pieces.at[slot, pl.ds(2 * quarter, 2 * quarter)],
                down.at[pl.ds(source * 2 * quarter, 2 * quarter)],
            )
        )
    copies = [pltpu.make_async_copy(*pair, sems.at[i]) for i, pair in enumerate(copies)]
    for copy in copies:
        copy.start()
    for copy in copies:
        copy.wait()


def place(pieces):
    features = pieces.shape[2]
    vmem = pl.BlockSpec(memory_space=pltpu.VMEM)
    return pl.pallas_call(
        place_kernel,
        out_shape=(
            jax.ShapeDtypeStruct((features, 4 * features), BF16),
            jax.ShapeDtypeStruct((4 * features, features), BF16),
        ),
        in_specs=[pl.BlockSpec(memory_space=pl.ANY)],
        out_specs=(vmem, vmem),
        scratch_shapes=[pltpu.SemaphoreType.DMA((3 * len(FOLDED),))],
    )(pieces)


def on_device(inputs, up_weight, down_weight, out_grad):
    own, features = inputs.shape
    side = lax.axis_index("k")
    half = up_weight.shape[1] // 2
    start = lax.axis_index("e") * half
    up_half = lax.dynamic_slice_in_dim(up_weight, start, half, 1)
    down_half = lax.dynamic_slice_in_dim(down_weight, start, half, 0)
    loss_scale = float(own * 64) ** (-0.5)

    def half_rows(which):
        return jnp.concatenate(
            [
                lax.dynamic_slice_in_dim(values, which * (own // 2), own // 2, 0)
                for values in (inputs, out_grad)
            ],
            axis=1,
        )

    kept, received = half_rows(side), other_core(half_rows(1 - side))
    up_half, down_half = after((up_half, down_half), received)
    both = jnp.concatenate([up_half[:, :features], up_half[:, features:]], axis=0)
    my_both = jnp.concatenate([down_half, both], axis=1)
    far_both = other_core(my_both)
    down_far = far_both[:, :features]
    up_far = jnp.concatenate([far_both[:features, features:], far_both[features:, features:]], axis=1)
    up_both = jnp.concatenate([up_half, up_far], axis=0)
    rows = jnp.concatenate(
        [
            kept[:, :features],
            received[:, :features],
            kept[:, features:],
            received[:, features:],
        ],
        axis=1,
    )
    rows = gather(after(rows, (up_half, down_half)), ("h", "e"))

    every_input = gather(rows[:, : 2 * features], "x")
    part = contract(every_input, up_both, ((1,), (0,))).astype(BF16)
    preact_sum = scatter_sum(part, "y")

    every_grad = after(gather(after(rows[:, 2 * features :], part), "x"), preact_sum)
    my_grad, far_grad = every_grad[:, :features], every_grad[:, features:]
    part = contract(my_grad, down_half, ((1,), (1,))) + contract(far_grad, down_far, ((1,), (1,)))
    part = part.astype(BF16)
    act_grad = scatter_sum(part, "y")

    preact = preact_sum.astype(BF16).astype(F32)
    act, act_grad, preact = lax.optimization_barrier(
        (gather(gelu_value(preact).astype(BF16), "y"), act_grad, preact)
    )
    far = contract(act, far_grad, ((0,), (0,))).astype(BF16)
    down_term = contract(act, my_grad, ((0,), (0,))) + other_core(far).astype(F32)
    down_term = (loss_scale * down_term).astype(BF16)
    down_piece = scatter_sum(down_term, "l").astype(BF16)

    hidden_grad = (act_grad * gelu_slope(preact)).astype(BF16)
    hidden = gather(after(hidden_grad, down_term), "y")
    far = contract(every_input[:, features:], hidden, ((0,), (0,))).astype(BF16)
    up_term = contract(every_input[:, :features], hidden, ((0,), (0,))) + other_core(far).astype(F32)
    up_term = (loss_scale * up_term).astype(BF16)

    act, hidden = after((act, hidden), up_term)
    far = other_core(feature_values(act, hidden, far_both))
    total = feature_values(act, hidden, my_both, far)
    total = total.reshape(16 * own, 2 * features)
    up_parts = after(lax.all_to_all(up_term, "l", 0, 0, tiled=True), total)
    up_piece = jnp.sum(up_parts.reshape(4, -1, half).astype(F32), axis=0).astype(BF16)
    piece = jnp.concatenate([up_piece[:, :features], up_piece[:, features:], down_piece], axis=0)
    packed = pack(piece)
    pieces = lax.all_gather(packed, ("e", "l"), axis_index_groups=[FOLDED])
    total, pieces = lax.optimization_barrier(
        (scatter_sum(after(total, packed), "x").astype(BF16), pieces)
    )
    up_grad, down_grad = place(unpack(pieces))
    total = total.reshape(2, 4, own // 2, 2 * features).transpose(1, 0, 2, 3)
    total = scatter_sum(total.reshape(4 * own, 2 * features), ("h", "e")).astype(BF16)
    total = after(total, (up_grad, down_grad))
    swapped = jnp.concatenate([total[own // 2 :], total[: own // 2]], axis=0)
    total = jnp.where(side == 0, total, swapped)
    return total[:, :features], total[:, features:], up_grad, down_grad


def solution(mesh):
    split = Mesh(mesh.devices.reshape(4, 2, 4, 2, 2, 4), ("x", "h", "y", "k", "e", "l"))
    rows = P(("e", "l", "x", "h"), ("y", "k"))
    up = P(("y", "k"), ("x", "h"))
    down = P(("x", "h"), ("y", "k"))
    return jax.shard_map(
        on_device,
        mesh=split,
        in_specs=(rows, up, down, rows),
        out_specs=(rows, rows, up, down),
        check_vma=False,
    )
```

```python
import jax
import jax.numpy as jnp
from jax import lax
from jax.experimental import pallas as pl
from jax.experimental.pallas import tpu as pltpu
from jax.sharding import Mesh
from jax.sharding import PartitionSpec as P

F32 = jnp.float32
BF16 = jnp.bfloat16
F16 = jnp.float16

FOLDED = [0, 2, 4, 6, 7, 5, 3, 1]


def gelu_value(wide):
    return 0.5 * wide * (1.0 + jax.scipy.special.erf(wide * 0.7071067811865476))


def gelu_slope(wide):
    return (
        0.5 * (1.0 + jax.scipy.special.erf(wide * 0.7071067811865476))
        + wide * jnp.exp(-0.5 * wide * wide) * 0.3989422804014327
    )


def contract(left, right, dims):
    return lax.dot_general(left, right, (dims, ((), ())), preferred_element_type=F32)


def scatter_sum(values, axis):
    count = lax.axis_size(axis)
    parts = lax.all_to_all(values, axis, 0, 0, tiled=True)
    parts = parts.reshape((count, parts.shape[0] // count) + parts.shape[1:])
    return jnp.sum(parts.astype(F32), axis=0)


def gather(values, axis):
    return lax.all_gather(values, axis, axis=0, tiled=True)


def other_core(values):
    return lax.ppermute(values, "k", [(0, 1), (1, 0)])


def after(values, earlier):
    return lax.optimization_barrier((values, earlier))[0]


def feature_kernel(act, hidden, weights, *rest):
    out = rest[-1]
    features = weights.shape[1] // 2
    rows = act.shape[0] // 16
    low, high = pl.ds(0, features), pl.ds(features, features)
    for columns in (low, high):
        if columns is low:
            values = contract(act[...], weights[:, low], ((1,), (0,)))
        else:
            values = contract(hidden[:, low], weights[low, high], ((1,), (1,)))
            values += contract(hidden[:, high], weights[high, high], ((1,), (1,)))
        values = values.astype(BF16)
        if len(rest) == 1:
            out[:, columns] = values
        else:
            for block in range(16):
                out[block, pl.ds(0, rows), columns] = values[block * rows : (block + 1) * rows]
    if len(rest) == 2:
        for block in range(16):
            out[block, pl.ds(rows, rows)] = rest[0][pl.ds(block * rows, rows)]


def feature_values(act, hidden, weights, *more):
    rows, depth = act.shape
    shape = (16, rows // 8, depth) if more else (rows, depth)
    return pl.pallas_call(
        feature_kernel,
        out_shape=jax.ShapeDtypeStruct(shape, BF16),
        cost_estimate=pl.CostEstimate(
            flops=2 * rows * depth * depth,
            bytes_accessed=6 * rows * depth + 2 * depth * depth,
            transcendentals=0,
        ),
    )(act, hidden, weights, *more)


def pack(piece):
    wide = piece.astype(F32)
    top = jnp.maximum(jnp.max(jnp.abs(wide)), 1e-37)
    power = jnp.clip(14.0 - jnp.ceil(jnp.log2(top)), -20.0, 120.0)
    scaled = (wide * jnp.exp2(power)).astype(F16)
    return jnp.concatenate([scaled, jnp.full((8, piece.shape[1]), power).astype(F16)], axis=0)


def unpack(packed):
    rows = packed.shape[1] - 8
    power = packed[:, rows:, :1].astype(F32)[:, :1]
    return (packed[:, :rows].astype(F32) * jnp.exp2(-power)).astype(BF16)


def place_kernel(pieces, up, down, sems):
    copies = []
    features = down.shape[1]
    quarter = features // 4
    for slot, source in enumerate(FOLDED):
        e, l = source // 4, source % 4
        for side in range(2):
            rows, cols = l * quarter, (2 * e + side) * features
            copies.append(
                (
                    pieces.at[slot, pl.ds(side * quarter, quarter)],
                    up.at[pl.ds(rows, quarter), pl.ds(cols, features)],
                )
            )
        copies.append(
            (
                pieces.at[slot, pl.ds(2 * quarter, 2 * quarter)],
                down.at[pl.ds(source * 2 * quarter, 2 * quarter)],
            )
        )
    copies = [pltpu.make_async_copy(*pair, sems.at[i]) for i, pair in enumerate(copies)]
    for copy in copies:
        copy.start()
    for copy in copies:
        copy.wait()


def place(pieces):
    features = pieces.shape[2]
    vmem = pl.BlockSpec(memory_space=pltpu.VMEM)
    return pl.pallas_call(
        place_kernel,
        out_shape=(
            jax.ShapeDtypeStruct((features, 4 * features), BF16),
            jax.ShapeDtypeStruct((4 * features, features), BF16),
        ),
        in_specs=[pl.BlockSpec(memory_space=pl.ANY)],
        out_specs=(vmem, vmem),
        scratch_shapes=[pltpu.SemaphoreType.DMA((3 * len(FOLDED),))],
    )(pieces)


def on_device(inputs, up_weight, down_weight, out_grad):
    own, features = inputs.shape
    side = lax.axis_index("k")
    half = up_weight.shape[1] // 2
    start = lax.axis_index("e") * half
    up_half = lax.dynamic_slice_in_dim(up_weight, start, half, 1)
    down_half = lax.dynamic_slice_in_dim(down_weight, start, half, 0)
    loss_scale = float(own * 64) ** (-0.5)

    def half_rows(which):
        return jnp.concatenate(
            [
                lax.dynamic_slice_in_dim(values, which * (own // 2), own // 2, 0)
                for values in (inputs, out_grad)
            ],
            axis=1,
        )

    kept, received = half_rows(side), other_core(half_rows(1 - side))
    up_half, down_half = after((up_half, down_half), received)
    both = jnp.concatenate([up_half[:, :features], up_half[:, features:]], axis=0)
    my_both = jnp.concatenate([down_half, both], axis=1)
    far_both = other_core(my_both)
    down_far = far_both[:, :features]
    up_far = jnp.concatenate([far_both[:features, features:], far_both[features:, features:]], axis=1)
    up_both = jnp.concatenate([up_half, up_far], axis=0)
    rows = jnp.concatenate(
        [
            kept[:, :features],
            received[:, :features],
            kept[:, features:],
            received[:, features:],
        ],
        axis=1,
    )
    rows = gather(after(rows, (up_half, down_half)), ("h", "e"))

    every_input = gather(rows[:, : 2 * features], "x")
    part = contract(every_input, up_both, ((1,), (0,))).astype(BF16)
    preact_sum = scatter_sum(part, "y")

    every_grad = after(gather(after(rows[:, 2 * features :], part), "x"), preact_sum)
    my_grad, far_grad = every_grad[:, :features], every_grad[:, features:]
    part = contract(my_grad, down_half, ((1,), (1,))) + contract(far_grad, down_far, ((1,), (1,)))
    part = part.astype(BF16)
    act_grad = scatter_sum(part, "y")

    preact = preact_sum.astype(BF16).astype(F32)
    act, act_grad, preact = lax.optimization_barrier(
        (gather(gelu_value(preact).astype(BF16), "y"), act_grad, preact)
    )
    far = contract(act, far_grad, ((0,), (0,))).astype(BF16)
    hidden_grad = (act_grad * gelu_slope(preact)).astype(BF16)
    my_grad = after(my_grad, hidden_grad)
    down_term = contract(act, my_grad, ((0,), (0,))) + other_core(far).astype(F32)
    down_term = (loss_scale * down_term).astype(BF16)
    down_piece = scatter_sum(down_term, "l").astype(BF16)

    hidden = gather(after(hidden_grad, down_term), "y")
    far = contract(every_input[:, features:], hidden, ((0,), (0,))).astype(BF16)
    up_term = contract(every_input[:, :features], hidden, ((0,), (0,))) + other_core(far).astype(F32)
    up_term = (loss_scale * up_term).astype(BF16)

    act, hidden = after((act, hidden), up_term)
    far = other_core(feature_values(act, hidden, far_both))
    total = feature_values(act, hidden, my_both, far)
    total = total.reshape(16 * own, 2 * features)
    up_parts = after(lax.all_to_all(up_term, "l", 0, 0, tiled=True), total)
    up_piece = jnp.sum(up_parts.reshape(4, -1, half).astype(F32), axis=0).astype(BF16)
    piece = jnp.concatenate([up_piece[:, :features], up_piece[:, features:], down_piece], axis=0)
    packed = pack(piece)
    pieces = lax.all_gather(packed, ("e", "l"), axis_index_groups=[FOLDED])
    total, pieces = lax.optimization_barrier(
        (scatter_sum(after(total, packed), "x").astype(BF16), pieces)
    )
    up_grad, down_grad = place(unpack(pieces))
    total = scatter_sum(total, ("h", "e")).astype(BF16)
    total = after(total, (up_grad, down_grad))
    swapped = jnp.concatenate([total[own // 2 :], total[: own // 2]], axis=0)
    total = jnp.where(side == 0, total, swapped)
    return total[:, :features], total[:, features:], up_grad, down_grad


def solution(mesh):
    split = Mesh(mesh.devices.reshape(4, 2, 4, 2, 2, 4), ("x", "h", "y", "k", "e", "l"))
    rows = P(("e", "l", "x", "h"), ("y", "k"))
    up = P(("y", "k"), ("x", "h"))
    down = P(("x", "h"), ("y", "k"))
    return jax.shard_map(
        on_device,
        mesh=split,
        in_specs=(rows, up, down, rows),
        out_specs=(rows, rows, up, down),
        check_vma=False,
    )
```

```python
import jax
import jax.numpy as jnp
from jax import lax
from jax.experimental import pallas as pl
from jax.experimental.pallas import tpu as pltpu
from jax.sharding import Mesh
from jax.sharding import PartitionSpec as P

F32 = jnp.float32
BF16 = jnp.bfloat16
F16 = jnp.float16

FOLDED = [0, 2, 4, 6, 7, 5, 3, 1]


def gelu_value(wide):
    return 0.5 * wide * (1.0 + jax.scipy.special.erf(wide * 0.7071067811865476))


def gelu_slope(wide):
    return (
        0.5 * (1.0 + jax.scipy.special.erf(wide * 0.7071067811865476))
        + wide * jnp.exp(-0.5 * wide * wide) * 0.3989422804014327
    )


def contract(left, right, dims):
    return lax.dot_general(left, right, (dims, ((), ())), preferred_element_type=F32)


def scatter_sum(values, axis):
    count = lax.axis_size(axis)
    parts = lax.all_to_all(values, axis, 0, 0, tiled=True)
    parts = parts.reshape((count, parts.shape[0] // count) + parts.shape[1:])
    return jnp.sum(parts.astype(F32), axis=0)


def gather(values, axis):
    return lax.all_gather(values, axis, axis=0, tiled=True)


def other_core(values):
    return lax.ppermute(values, "k", [(0, 1), (1, 0)])


def after(values, earlier):
    return lax.optimization_barrier((values, earlier))[0]


def feature_kernel(act, hidden, weights, *rest):
    out = rest[-1]
    features = weights.shape[1] // 2
    rows = act.shape[0] // 4
    low, high = pl.ds(0, features), pl.ds(features, features)
    for columns in (low, high):
        if columns is low:
            values = contract(act[...], weights[:, low], ((1,), (0,)))
        else:
            values = contract(hidden[:, low], weights[low, high], ((1,), (1,)))
            values += contract(hidden[:, high], weights[high, high], ((1,), (1,)))
        values = values.astype(BF16)
        if len(rest) == 1:
            out[:, columns] = values
        else:
            for block in range(4):
                out[block, pl.ds(0, rows), columns] = values[block * rows : (block + 1) * rows]
    if len(rest) == 2:
        for block in range(4):
            out[block, pl.ds(rows, rows)] = rest[0][pl.ds(block * rows, rows)]


def feature_values(act, hidden, weights, *more):
    rows, depth = act.shape
    shape = (4, rows // 2, depth) if more else (rows, depth)
    return pl.pallas_call(
        feature_kernel,
        out_shape=jax.ShapeDtypeStruct(shape, BF16),
        cost_estimate=pl.CostEstimate(
            flops=2 * rows * depth * depth,
            bytes_accessed=6 * rows * depth + 2 * depth * depth,
            transcendentals=0,
        ),
    )(act, hidden, weights, *more)


def pack(piece):
    wide = piece.astype(F32)
    top = jnp.maximum(jnp.max(jnp.abs(wide)), 1e-37)
    power = jnp.clip(14.0 - jnp.ceil(jnp.log2(top)), -20.0, 120.0)
    scaled = (wide * jnp.exp2(power)).astype(F16)
    return jnp.concatenate([scaled, jnp.full((8, piece.shape[1]), power).astype(F16)], axis=0)


def unpack(packed):
    rows = packed.shape[1] - 8
    power = packed[:, rows:, :1].astype(F32)[:, :1]
    return (packed[:, :rows].astype(F32) * jnp.exp2(-power)).astype(BF16)


def place_kernel(pieces, up, down, sems):
    copies = []
    features = down.shape[1]
    quarter = features // 4
    for slot, source in enumerate(FOLDED):
        e, l = source // 4, source % 4
        for side in range(2):
            rows, cols = l * quarter, (2 * e + side) * features
            copies.append(
                (
                    pieces.at[slot, pl.ds(side * quarter, quarter)],
                    up.at[pl.ds(rows, quarter), pl.ds(cols, features)],
                )
            )
        copies.append(
            (
                pieces.at[slot, pl.ds(2 * quarter, 2 * quarter)],
                down.at[pl.ds(source * 2 * quarter, 2 * quarter)],
            )
        )
    copies = [pltpu.make_async_copy(*pair, sems.at[i]) for i, pair in enumerate(copies)]
    for copy in copies:
        copy.start()
    for copy in copies:
        copy.wait()


def place(pieces):
    features = pieces.shape[2]
    vmem = pl.BlockSpec(memory_space=pltpu.VMEM)
    return pl.pallas_call(
        place_kernel,
        out_shape=(
            jax.ShapeDtypeStruct((features, 4 * features), BF16),
            jax.ShapeDtypeStruct((4 * features, features), BF16),
        ),
        in_specs=[pl.BlockSpec(memory_space=pl.ANY)],
        out_specs=(vmem, vmem),
        scratch_shapes=[pltpu.SemaphoreType.DMA((3 * len(FOLDED),))],
    )(pieces)


def on_device(inputs, up_weight, down_weight, out_grad):
    own, features = inputs.shape
    side = lax.axis_index("k")
    half = up_weight.shape[1] // 2
    start = lax.axis_index("e") * half
    up_half = lax.dynamic_slice_in_dim(up_weight, start, half, 1)
    down_half = lax.dynamic_slice_in_dim(down_weight, start, half, 0)
    loss_scale = float(own * 64) ** (-0.5)

    def half_rows(which):
        return jnp.concatenate(
            [
                lax.dynamic_slice_in_dim(values, which * (own // 2), own // 2, 0)
                for values in (inputs, out_grad)
            ],
            axis=1,
        )

    kept, received = half_rows(side), other_core(half_rows(1 - side))
    up_half, down_half = after((up_half, down_half), received)
    both = jnp.concatenate([up_half[:, :features], up_half[:, features:]], axis=0)
    my_both = jnp.concatenate([down_half, both], axis=1)
    far_both = other_core(my_both)
    down_far = far_both[:, :features]
    up_far = jnp.concatenate([far_both[:features, features:], far_both[features:, features:]], axis=1)
    up_both = jnp.concatenate([up_half, up_far], axis=0)
    rows = jnp.concatenate(
        [
            kept[:, :features],
            received[:, :features],
            kept[:, features:],
            received[:, features:],
        ],
        axis=1,
    )
    rows = gather(after(rows, (up_half, down_half)), ("h", "e"))

    every_input = gather(rows[:, : 2 * features], "x")
    part = contract(every_input, up_both, ((1,), (0,))).astype(BF16)
    preact_sum = scatter_sum(part, "y")

    every_grad = after(gather(after(rows[:, 2 * features :], part), "x"), preact_sum)
    my_grad, far_grad = every_grad[:, :features], every_grad[:, features:]
    part = contract(my_grad, down_half, ((1,), (1,))) + contract(far_grad, down_far, ((1,), (1,)))
    part = part.astype(BF16)
    act_grad = scatter_sum(part, "y")

    preact = preact_sum.astype(BF16).astype(F32)
    act, act_grad, preact = lax.optimization_barrier(
        (gather(gelu_value(preact).astype(BF16), "y"), act_grad, preact)
    )
    far = contract(act, far_grad, ((0,), (0,))).astype(BF16)
    down_term = contract(act, my_grad, ((0,), (0,))) + other_core(far).astype(F32)
    down_term = (loss_scale * down_term).astype(BF16)
    down_piece = scatter_sum(down_term, "l").astype(BF16)

    hidden_grad = (act_grad * gelu_slope(preact)).astype(BF16)
    hidden = gather(after(hidden_grad, down_term), "y")
    far = contract(every_input[:, features:], hidden, ((0,), (0,))).astype(BF16)
    up_term = contract(every_input[:, :features], hidden, ((0,), (0,))) + other_core(far).astype(F32)
    up_term = (loss_scale * up_term).astype(BF16)

    act, hidden = after((act, hidden), up_term)
    far = other_core(feature_values(act, hidden, far_both))
    total = feature_values(act, hidden, my_both, far)
    total = total.reshape(16 * own, 2 * features)
    up_parts = after(lax.all_to_all(up_term, "l", 0, 0, tiled=True), total)
    up_piece = jnp.sum(up_parts.reshape(4, -1, half).astype(F32), axis=0).astype(BF16)
    piece = jnp.concatenate([up_piece[:, :features], up_piece[:, features:], down_piece], axis=0)
    packed = pack(piece)
    pieces = lax.all_gather(packed, ("e", "l"), axis_index_groups=[FOLDED])
    total, pieces = lax.optimization_barrier(
        (scatter_sum(after(total, packed), "x").astype(BF16), pieces)
    )
    up_grad, down_grad = place(unpack(pieces))
    total = total.reshape(2, 4, own // 2, 2 * features).transpose(1, 0, 2, 3)
    total = scatter_sum(total.reshape(4 * own, 2 * features), ("h", "e")).astype(BF16)
    total = after(total, (up_grad, down_grad))
    swapped = jnp.concatenate([total[own // 2 :], total[: own // 2]], axis=0)
    total = jnp.where(side == 0, total, swapped)
    return total[:, :features], total[:, features:], up_grad, down_grad


def solution(mesh):
    split = Mesh(mesh.devices.reshape(4, 2, 4, 2, 2, 4), ("x", "h", "y", "k", "e", "l"))
    rows = P(("e", "l", "x", "h"), ("y", "k"))
    up = P(("y", "k"), ("x", "h"))
    down = P(("x", "h"), ("y", "k"))
    return jax.shard_map(
        on_device,
        mesh=split,
        in_specs=(rows, up, down, rows),
        out_specs=(rows, rows, up, down),
        check_vma=False,
    )
```

```python
import jax
import jax.numpy as jnp
from jax import lax
from jax.experimental import pallas as pl
from jax.experimental.pallas import tpu as pltpu
from jax.sharding import Mesh
from jax.sharding import PartitionSpec as P

F32 = jnp.float32
BF16 = jnp.bfloat16
F16 = jnp.float16

FOLDED = [0, 2, 4, 6, 7, 5, 3, 1]


def gelu_value(wide):
    return 0.5 * wide * (1.0 + jax.scipy.special.erf(wide * 0.7071067811865476))


def gelu_slope(wide):
    return (
        0.5 * (1.0 + jax.scipy.special.erf(wide * 0.7071067811865476))
        + wide * jnp.exp(-0.5 * wide * wide) * 0.3989422804014327
    )


def contract(left, right, dims):
    return lax.dot_general(left, right, (dims, ((), ())), preferred_element_type=F32)


def scatter_sum(values, axis):
    count = lax.axis_size(axis)
    parts = lax.all_to_all(values, axis, 0, 0, tiled=True)
    parts = parts.reshape((count, parts.shape[0] // count) + parts.shape[1:])
    return jnp.sum(parts.astype(F32), axis=0)


def gather(values, axis):
    return lax.all_gather(values, axis, axis=0, tiled=True)


def other_core(values):
    return lax.ppermute(values, "k", [(0, 1), (1, 0)])


def after(values, earlier):
    return lax.optimization_barrier((values, earlier))[0]


def feature_kernel(act, hidden, weights, *rest):
    out = rest[0] if len(rest) == 1 else rest[1]
    features = weights.shape[1] // 2
    rows = act.shape[0] // 4
    copies = []
    if len(rest) == 3:
        for block in range(4):
            source, target = rest[0].at[pl.ds(block * rows, rows)], out.at[block, pl.ds(rows, rows)]
            copies.append(pltpu.make_async_copy(source, target, rest[2].at[block]))
    for copy in copies:
        copy.start()
    low, high = pl.ds(0, features), pl.ds(features, features)
    for columns in (low, high):
        if columns is low:
            values = contract(act[...], weights[:, low], ((1,), (0,)))
        else:
            values = contract(hidden[:, low], weights[low, high], ((1,), (1,)))
            values += contract(hidden[:, high], weights[high, high], ((1,), (1,)))
        values = values.astype(BF16)
        if len(rest) == 1:
            out[:, columns] = values
        else:
            for block in range(4):
                out[block, pl.ds(0, rows), columns] = values[block * rows : (block + 1) * rows]
    for copy in copies:
        copy.wait()


def feature_values(act, hidden, weights, *more):
    rows, depth = act.shape
    shape = (4, rows // 2, depth) if more else (rows, depth)
    vmem = pl.BlockSpec(memory_space=pltpu.VMEM)
    return pl.pallas_call(
        feature_kernel,
        out_shape=jax.ShapeDtypeStruct(shape, BF16),
        in_specs=[vmem] * 3 + [pl.BlockSpec(memory_space=pl.ANY)] * len(more),
        out_specs=vmem,
        scratch_shapes=[pltpu.SemaphoreType.DMA((4,))] * len(more),
        cost_estimate=pl.CostEstimate(
            flops=2 * rows * depth * depth,
            bytes_accessed=6 * rows * depth + 2 * depth * depth,
            transcendentals=0,
        ),
    )(act, hidden, weights, *more)


def pack(piece):
    wide = piece.astype(F32)
    top = jnp.maximum(jnp.max(jnp.abs(wide)), 1e-37)
    power = jnp.clip(14.0 - jnp.ceil(jnp.log2(top)), -20.0, 120.0)
    scaled = (wide * jnp.exp2(power)).astype(F16)
    return jnp.concatenate([scaled, jnp.full((16, piece.shape[1]), power).astype(F16)], axis=0)


def unpack(packed):
    rows = packed.shape[1] - 16
    power = packed[:, rows:, :1].astype(F32)[:, :1]
    return (packed[:, :rows].astype(F32) * jnp.exp2(-power)).astype(BF16)


def place_kernel(pieces, up, down, sems):
    copies = []
    features = down.shape[1]
    quarter = features // 4
    for slot, source in enumerate(FOLDED):
        e, l = source // 4, source % 4
        for side in range(2):
            rows, cols = l * quarter, (2 * e + side) * features
            copies.append(
                (
                    pieces.at[slot, pl.ds(side * quarter, quarter)],
                    up.at[pl.ds(rows, quarter), pl.ds(cols, features)],
                )
            )
        copies.append(
            (
                pieces.at[slot, pl.ds(2 * quarter, 2 * quarter)],
                down.at[pl.ds(source * 2 * quarter, 2 * quarter)],
            )
        )
    copies = [pltpu.make_async_copy(*pair, sems.at[i]) for i, pair in enumerate(copies)]
    for copy in copies:
        copy.start()
    for copy in copies:
        copy.wait()


def place(pieces):
    features = pieces.shape[2]
    vmem = pl.BlockSpec(memory_space=pltpu.VMEM)
    return pl.pallas_call(
        place_kernel,
        out_shape=(
            jax.ShapeDtypeStruct((features, 4 * features), BF16),
            jax.ShapeDtypeStruct((4 * features, features), BF16),
        ),
        in_specs=[pl.BlockSpec(memory_space=pl.ANY)],
        out_specs=(vmem, vmem),
        scratch_shapes=[pltpu.SemaphoreType.DMA((3 * len(FOLDED),))],
    )(pieces)


def on_device(inputs, up_weight, down_weight, out_grad):
    own, features = inputs.shape
    side = lax.axis_index("k")
    half = up_weight.shape[1] // 2
    start = lax.axis_index("e") * half
    up_half = lax.dynamic_slice_in_dim(up_weight, start, half, 1)
    down_half = lax.dynamic_slice_in_dim(down_weight, start, half, 0)
    loss_scale = float(own * 64) ** (-0.5)

    def half_rows(which):
        return jnp.concatenate(
            [
                lax.dynamic_slice_in_dim(values, which * (own // 2), own // 2, 0)
                for values in (inputs, out_grad)
            ],
            axis=1,
        )

    kept, received = half_rows(side), other_core(half_rows(1 - side))
    up_half, down_half = after((up_half, down_half), received)
    both = jnp.concatenate([up_half[:, :features], up_half[:, features:]], axis=0)
    my_both = jnp.concatenate([down_half, both], axis=1)
    far_both = other_core(my_both)
    down_far = far_both[:, :features]
    up_far = jnp.concatenate([far_both[:features, features:], far_both[features:, features:]], axis=1)
    up_both = jnp.concatenate([up_half, up_far], axis=0)
    rows = jnp.concatenate(
        [
            kept[:, :features],
            received[:, :features],
            kept[:, features:],
            received[:, features:],
        ],
        axis=1,
    )
    rows = gather(after(rows, (up_half, down_half)), ("h", "e"))

    every_input = gather(rows[:, : 2 * features], "x")
    part = contract(every_input, up_both, ((1,), (0,))).astype(BF16)
    preact_sum = scatter_sum(part, "y")

    every_grad = after(gather(after(rows[:, 2 * features :], part), "x"), preact_sum)
    my_grad, far_grad = every_grad[:, :features], every_grad[:, features:]
    part = contract(my_grad, down_half, ((1,), (1,))) + contract(far_grad, down_far, ((1,), (1,)))
    part = part.astype(BF16)
    act_grad = scatter_sum(part, "y")

    preact = preact_sum.astype(BF16).astype(F32)
    act, act_grad, preact = lax.optimization_barrier(
        (gather(gelu_value(preact).astype(BF16), "y"), act_grad, preact)
    )
    far = contract(act, far_grad, ((0,), (0,))).astype(BF16)
    down_term = contract(act, my_grad, ((0,), (0,))) + other_core(far).astype(F32)
    down_term = (loss_scale * down_term).astype(BF16)
    down_piece = scatter_sum(down_term, "l").astype(BF16)

    hidden_grad = (act_grad * gelu_slope(preact)).astype(BF16)
    hidden = gather(after(hidden_grad, down_term), "y")
    far = contract(every_input[:, features:], hidden, ((0,), (0,))).astype(BF16)
    up_term = contract(every_input[:, :features], hidden, ((0,), (0,))) + other_core(far).astype(F32)
    up_term = (loss_scale * up_term).astype(BF16)

    act, hidden = after((act, hidden), up_term)
    far = other_core(feature_values(act, hidden, far_both))
    total = feature_values(act, hidden, my_both, far)
    total = total.reshape(16 * own, 2 * features)
    up_parts = after(lax.all_to_all(up_term, "l", 0, 0, tiled=True), total)
    up_piece = jnp.sum(up_parts.reshape(4, -1, half).astype(F32), axis=0).astype(BF16)
    piece = jnp.concatenate([up_piece[:, :features], up_piece[:, features:], down_piece], axis=0)
    packed = pack(piece)
    pieces = lax.all_gather(packed, ("e", "l"), axis_index_groups=[FOLDED])
    total, pieces = lax.optimization_barrier(
        (scatter_sum(after(total, packed), "x").astype(BF16), pieces)
    )
    up_grad, down_grad = place(unpack(pieces))
    total = total.reshape(2, 4, own // 2, 2 * features).transpose(1, 0, 2, 3)
    total = scatter_sum(total.reshape(4 * own, 2 * features), ("h", "e")).astype(BF16)
    total = after(total, (up_grad, down_grad))
    swapped = jnp.concatenate([total[own // 2 :], total[: own // 2]], axis=0)
    total = jnp.where(side == 0, total, swapped)
    return total[:, :features], total[:, features:], up_grad, down_grad


def solution(mesh):
    split = Mesh(mesh.devices.reshape(4, 2, 4, 2, 2, 4), ("x", "h", "y", "k", "e", "l"))
    rows = P(("e", "l", "x", "h"), ("y", "k"))
    up = P(("y", "k"), ("x", "h"))
    down = P(("x", "h"), ("y", "k"))
    return jax.shard_map(
        on_device,
        mesh=split,
        in_specs=(rows, up, down, rows),
        out_specs=(rows, rows, up, down),
        check_vma=False,
    )
```

```python
import jax
import jax.numpy as jnp
from jax import lax
from jax.experimental import pallas as pl
from jax.experimental.pallas import tpu as pltpu
from jax.sharding import Mesh
from jax.sharding import PartitionSpec as P

F32 = jnp.float32
BF16 = jnp.bfloat16
F16 = jnp.float16

FOLDED = [0, 2, 4, 6, 7, 5, 3, 1]


def gelu_value(wide):
    return 0.5 * wide * (1.0 + jax.scipy.special.erf(wide * 0.7071067811865476))


def gelu_slope(wide):
    return (
        0.5 * (1.0 + jax.scipy.special.erf(wide * 0.7071067811865476))
        + wide * jnp.exp(-0.5 * wide * wide) * 0.3989422804014327
    )


def contract(left, right, dims):
    return lax.dot_general(left, right, (dims, ((), ())), preferred_element_type=F32)


def scatter_sum(values, axis):
    count = lax.axis_size(axis)
    parts = lax.all_to_all(values, axis, 0, 0, tiled=True)
    parts = parts.reshape((count, parts.shape[0] // count) + parts.shape[1:])
    return jnp.sum(parts.astype(F32), axis=0)


def gather(values, axis):
    return lax.all_gather(values, axis, axis=0, tiled=True)


def other_core(values):
    return lax.ppermute(values, "k", [(0, 1), (1, 0)])


def after(values, earlier):
    return lax.optimization_barrier((values, earlier))[0]


def feature_kernel(act, hidden, weights, *rest):
    out = rest[0] if len(rest) == 1 else rest[1]
    features = weights.shape[1] // 2
    rows = act.shape[0] // 16
    copies = []
    if len(rest) == 3:
        for block in range(16):
            source, target = rest[0].at[pl.ds(block * rows, rows)], out.at[block, pl.ds(rows, rows)]
            copies.append(pltpu.make_async_copy(source, target, rest[2].at[block]))
    for copy in copies:
        copy.start()
    low, high = pl.ds(0, features), pl.ds(features, features)
    for columns in (low, high):
        if columns is low:
            values = contract(act[...], weights[:, low], ((1,), (0,)))
        else:
            values = contract(hidden[:, low], weights[low, high], ((1,), (1,)))
            values += contract(hidden[:, high], weights[high, high], ((1,), (1,)))
        values = values.astype(BF16)
        if len(rest) == 1:
            out[:, columns] = values
        else:
            for block in range(16):
                out[block, pl.ds(0, rows), columns] = values[block * rows : (block + 1) * rows]
    for copy in copies:
        copy.wait()


def feature_values(act, hidden, weights, *more):
    rows, depth = act.shape
    shape = (16, rows // 8, depth) if more else (rows, depth)
    vmem = pl.BlockSpec(memory_space=pltpu.VMEM)
    return pl.pallas_call(
        feature_kernel,
        out_shape=jax.ShapeDtypeStruct(shape, BF16),
        in_specs=[vmem] * 3 + [pl.BlockSpec(memory_space=pl.ANY)] * len(more),
        out_specs=vmem,
        scratch_shapes=[pltpu.SemaphoreType.DMA((16,))] * len(more),
        cost_estimate=pl.CostEstimate(
            flops=2 * rows * depth * depth,
            bytes_accessed=6 * rows * depth + 2 * depth * depth,
            transcendentals=0,
        ),
    )(act, hidden, weights, *more)


def pack(piece):
    wide = piece.astype(F32)
    top = jnp.maximum(jnp.max(jnp.abs(wide)), 1e-37)
    power = jnp.clip(14.0 - jnp.ceil(jnp.log2(top)), -20.0, 120.0)
    scaled = (wide * jnp.exp2(power)).astype(F16)
    return jnp.concatenate([scaled, jnp.full((16, piece.shape[1]), power).astype(F16)], axis=0)


def unpack(packed):
    rows = packed.shape[1] - 16
    power = packed[:, rows:, :1].astype(F32)[:, :1]
    return (packed[:, :rows].astype(F32) * jnp.exp2(-power)).astype(BF16)


def place_kernel(pieces, up, down, sems):
    copies = []
    features = down.shape[1]
    quarter = features // 4
    for slot, source in enumerate(FOLDED):
        e, l = source // 4, source % 4
        for side in range(2):
            rows, cols = l * quarter, (2 * e + side) * features
            copies.append(
                (
                    pieces.at[slot, pl.ds(side * quarter, quarter)],
                    up.at[pl.ds(rows, quarter), pl.ds(cols, features)],
                )
            )
        copies.append(
            (
                pieces.at[slot, pl.ds(2 * quarter, 2 * quarter)],
                down.at[pl.ds(source * 2 * quarter, 2 * quarter)],
            )
        )
    copies = [pltpu.make_async_copy(*pair, sems.at[i]) for i, pair in enumerate(copies)]
    for copy in copies:
        copy.start()
    for copy in copies:
        copy.wait()


def place(pieces):
    features = pieces.shape[2]
    vmem = pl.BlockSpec(memory_space=pltpu.VMEM)
    return pl.pallas_call(
        place_kernel,
        out_shape=(
            jax.ShapeDtypeStruct((features, 4 * features), BF16),
            jax.ShapeDtypeStruct((4 * features, features), BF16),
        ),
        in_specs=[pl.BlockSpec(memory_space=pl.ANY)],
        out_specs=(vmem, vmem),
        scratch_shapes=[pltpu.SemaphoreType.DMA((3 * len(FOLDED),))],
    )(pieces)


def on_device(inputs, up_weight, down_weight, out_grad):
    own, features = inputs.shape
    side = lax.axis_index("k")
    half = up_weight.shape[1] // 2
    start = lax.axis_index("e") * half
    up_half = lax.dynamic_slice_in_dim(up_weight, start, half, 1)
    down_half = lax.dynamic_slice_in_dim(down_weight, start, half, 0)
    loss_scale = float(own * 64) ** (-0.5)

    def half_rows(which):
        return jnp.concatenate(
            [
                lax.dynamic_slice_in_dim(values, which * (own // 2), own // 2, 0)
                for values in (inputs, out_grad)
            ],
            axis=1,
        )

    kept, received = half_rows(side), other_core(half_rows(1 - side))
    up_half, down_half = after((up_half, down_half), received)
    both = jnp.concatenate([up_half[:, :features], up_half[:, features:]], axis=0)
    my_both = jnp.concatenate([down_half, both], axis=1)
    far_both = other_core(my_both)
    down_far = far_both[:, :features]
    up_far = jnp.concatenate([far_both[:features, features:], far_both[features:, features:]], axis=1)
    up_both = jnp.concatenate([up_half, up_far], axis=0)
    rows = jnp.concatenate(
        [
            kept[:, :features],
            received[:, :features],
            kept[:, features:],
            received[:, features:],
        ],
        axis=1,
    )
    rows = gather(after(rows, (up_half, down_half)), ("h", "e"))

    every_input = gather(rows[:, : 2 * features], "x")
    part = contract(every_input, up_both, ((1,), (0,))).astype(BF16)
    preact_sum = scatter_sum(part, "y")

    every_grad = after(gather(after(rows[:, 2 * features :], part), "x"), preact_sum)
    my_grad, far_grad = every_grad[:, :features], every_grad[:, features:]
    part = contract(my_grad, down_half, ((1,), (1,))) + contract(far_grad, down_far, ((1,), (1,)))
    part = part.astype(BF16)
    act_grad = scatter_sum(part, "y")

    preact = preact_sum.astype(BF16).astype(F32)
    act, act_grad, preact = lax.optimization_barrier(
        (gather(gelu_value(preact).astype(BF16), "y"), act_grad, preact)
    )
    far = contract(act, far_grad, ((0,), (0,))).astype(BF16)
    down_term = contract(act, my_grad, ((0,), (0,))) + other_core(far).astype(F32)
    down_term = (loss_scale * down_term).astype(BF16)
    down_piece = scatter_sum(down_term, "l").astype(BF16)

    hidden_grad = (act_grad * gelu_slope(preact)).astype(BF16)
    hidden = gather(after(hidden_grad, down_term), "y")
    far = contract(every_input[:, features:], hidden, ((0,), (0,))).astype(BF16)
    up_term = contract(every_input[:, :features], hidden, ((0,), (0,))) + other_core(far).astype(F32)
    up_term = (loss_scale * up_term).astype(BF16)

    act, hidden = after((act, hidden), up_term)
    far = other_core(feature_values(act, hidden, far_both))
    total = feature_values(act, hidden, my_both, far)
    total = total.reshape(16 * own, 2 * features)
    up_parts = after(lax.all_to_all(up_term, "l", 0, 0, tiled=True), total)
    up_piece = jnp.sum(up_parts.reshape(4, -1, half).astype(F32), axis=0).astype(BF16)
    piece = jnp.concatenate([up_piece[:, :features], up_piece[:, features:], down_piece], axis=0)
    packed = pack(piece)
    pieces = lax.all_gather(packed, ("e", "l"), axis_index_groups=[FOLDED])
    total, pieces = lax.optimization_barrier(
        (scatter_sum(after(total, packed), "x").astype(BF16), pieces)
    )
    up_grad, down_grad = place(unpack(pieces))
    total = scatter_sum(total, ("h", "e")).astype(BF16)
    total = after(total, (up_grad, down_grad))
    swapped = jnp.concatenate([total[own // 2 :], total[: own // 2]], axis=0)
    total = jnp.where(side == 0, total, swapped)
    return total[:, :features], total[:, features:], up_grad, down_grad


def solution(mesh):
    split = Mesh(mesh.devices.reshape(4, 2, 4, 2, 2, 4), ("x", "h", "y", "k", "e", "l"))
    rows = P(("e", "l", "x", "h"), ("y", "k"))
    up = P(("y", "k"), ("x", "h"))
    down = P(("x", "h"), ("y", "k"))
    return jax.shard_map(
        on_device,
        mesh=split,
        in_specs=(rows, up, down, rows),
        out_specs=(rows, rows, up, down),
        check_vma=False,
    )
```
